32 devices in a mesh: grp: 4 (over y, x), tile: 8 (over z, core).
Axes of the slice: x: 2, y: 2, z: 4, core: 2. Of those that a mesh axis runs over, the one named last changes fastest.
Arguments:
- rhs_fiber: float32 [2048, 256], P(('grp', 'tile')), may hold values from -6 to 6
- rhs_body: float32 [400, 4608], P('grp', 'tile'), may hold values from -6 to 6
- fiber_ops: bfloat16 [2048, 256, 256], P(('grp', 'tile')), may hold values from -0.375 to 0.375
- body_op: bfloat16 [4608, 4608], P('tile'), may hold values from -0.09375 to 0.09375
- positions: float32 [3, 131072], P(None, ('grp', 'tile')), may hold values from 0 to 1
- send_order: int32 [32, 4096], P(('grp', 'tile')), may hold values from 0 to 4095, each once within a row
- leaf_order: int32 [32, 4096], P(('grp', 'tile')), may hold values from 0 to 4095, each once within a row
- neighbours: int32 [1024, 2], P(('grp', 'tile')), may hold values 0 or 1
- attach_nucleus: int32 [2048], P(('grp', 'tile')), may hold values from 0 to 99
- attach_node: int32 [2048], P(('grp', 'tile')), may hold values from 0 to 1535
Outputs:
- sol_fiber: float32 [2048, 256], P(('grp', 'tile'))
- sol_body: float32 [400, 4608], P('grp', 'tile')
The draws below stay inside these ranges and needn't reach their ends.
Inputs may be any that keep to these rules, and one draw needn't show every extreme that they name: `send_order`: each row is a permutation of the device's 4096 node positions, so each device sends exactly 4096 / 8 nodes to every device of its group. `leaf_order`: each row is a permutation of the device's 4096 received slots.
All inputs are finite; a program needn't handle non-finite values. No bound on the sum of `neighbours` on one device may be relied on, other than what follows from the above.
Results may differ from the reference program's by a relative error of at most 0.002.
Values may be sent and summed in bfloat16 or wider, within the bound.
A program may use at most 128 MiB of HBM per device.

```python
import math
import jax
import jax.numpy as jnp
from jax import lax

FNODES = 64
BNODES = 1536
FIB_DEV = 64
NUC_GRP = 100
LEAF_PTS = 128
ITERS = 3
ORDER = 256
BCOLS = 4608
NODE_DEV = 4096
FIBERS = 2048
NODES = 131072
NUCLEI = 400
LEAVES = 1024
N_GRP = 4
N_TILE = 8


def plant(entries, key, low, high):
    dims = entries.shape
    index_at = [jax.random.randint(jax.random.fold_in(key, axis), (), 0, dims[axis]) for axis in range(len(dims))]
    entries = entries.at[tuple(index_at)].set(low)
    longest = dims.index(max(dims))
    index_at[longest] = (index_at[longest] + 1) % dims[longest]
    return entries.at[tuple(index_at)].set(high)


def block_scale(key, shape, cuts, low, top_value):
    def one(axis_at, blocks):
        heights = jax.random.uniform(jax.random.fold_in(jax.random.fold_in(key, 6), axis_at), (blocks,), jnp.float32, low / len(cuts), top_value / len(cuts))
        return jnp.repeat(jnp.exp(heights), shape[axis_at] // blocks).reshape((-1,) + (1,) * (len(shape) - axis_at - 1))

    factor_of = one(*cuts[0])
    for cut in cuts[1:]:
        factor_of = factor_of * one(*cut)
    return factor_of


def normal_values(own_key, shape, deviation, bound, shards=(), kind=jnp.bfloat16):
    loudness = block_scale(own_key, shape, shards, -0.22, 0.18) if shards else 1.0
    values = jax.random.normal(own_key, shape, jnp.float32) * deviation * loudness
    return jnp.minimum(jnp.maximum(values, -bound), bound).astype(kind)


def setup_inputs(seed: int = 0) -> dict:
    arg_keys = jax.random.split(jax.random.key(seed), 11)
    rhs_fiber = normal_values(arg_keys[0], (FIBERS, ORDER), 1.0, 6.0, ((0, 32),), jnp.float32)
    rhs_body = normal_values(arg_keys[1], (NUCLEI, BCOLS), 1.0, 6.0, ((0, 4), (1, 8)), jnp.float32)
    fiber_ops = normal_values(arg_keys[2], (FIBERS, ORDER, ORDER), ORDER ** -0.5, 0.375, ((0, 32),))
    body_op = normal_values(arg_keys[3], (BCOLS, BCOLS), BCOLS ** -0.5, 0.09375, ((0, 8),))
    positions = jnp.clip(1.0 * jax.random.uniform(arg_keys[4], (3, NODES), jnp.float32) ** block_scale(arg_keys[4], (3, NODES), ((1, 32),), -0.2, 0.2), 0.0, 1.0)
    send_order = jax.vmap(lambda own: jax.random.permutation(own, NODE_DEV))(jax.random.split(arg_keys[5], (N_GRP * N_TILE))).reshape((N_GRP * N_TILE, NODE_DEV)).astype(jnp.int32)
    leaf_order = jax.vmap(lambda own: jax.random.permutation(own, NODE_DEV))(jax.random.split(arg_keys[6], (N_GRP * N_TILE))).reshape((N_GRP * N_TILE, NODE_DEV)).astype(jnp.int32)
    neighbours = plant((jax.random.randint(arg_keys[7], (LEAVES, 2), 0, 4) < 3).astype(jnp.int32), jax.random.fold_in(arg_keys[7], 1), 0, 1)
    attach_nucleus = plant(jax.random.randint(arg_keys[8], (FIBERS,), 0, NUC_GRP), jax.random.fold_in(arg_keys[8], 1), 0, NUC_GRP - 1).astype(jnp.int32)
    attach_node = plant(jax.random.randint(arg_keys[9], (FIBERS,), 0, BNODES), jax.random.fold_in(arg_keys[9], 1), 0, BNODES - 1).astype(jnp.int32)
    return dict(rhs_fiber=rhs_fiber, rhs_body=rhs_body, fiber_ops=fiber_ops, body_op=body_op, positions=positions, send_order=send_order, leaf_order=leaf_order, neighbours=neighbours, attach_nucleus=attach_nucleus, attach_node=attach_node)


kappa_coef = 0.5
eps_square = 0.0025
stokes_coef = 1.0 / (16.0 * math.pi)

def stokes_block(target_pos, source_pos, source_force):
    delta_pos = target_pos[:, :, :, None] - source_pos[:, :, None, :]
    dist_square = lax.optimization_barrier(jnp.sum(delta_pos * delta_pos, axis=1))
    along_force = lax.optimization_barrier(jnp.sum(delta_pos * source_force[:, :, None, :], axis=1))
    inv_root = lax.rsqrt(dist_square + eps_square)
    inv_cube = inv_root * inv_root * inv_root
    terms = (source_force[:, :, None, :] * (dist_square + 2.0 * eps_square)[:, None] + delta_pos * along_force[:, None]) * inv_cube[:, None]
    return stokes_coef * lax.optimization_barrier(jnp.sum(terms, axis=3))

def window_velocity(leaf_pos, pos_left, pos_right, leaf_force, force_left, force_right, leaf_masks, block_size):
    source_pos = jnp.concatenate([pos_left, leaf_pos, pos_right], axis=2)
    source_force = jnp.concatenate([force_left * leaf_masks[:, 0, None, None], leaf_force, force_right * leaf_masks[:, 1, None, None]], axis=2)
    leaf_count = leaf_pos.shape[0]

    def shaped(array):
        return array.reshape((leaf_count // block_size, block_size) + array.shape[1:])

    def one_block(pieces):
        return stokes_block(pieces[0], pieces[1], pieces[2])
    result = lax.map(one_block, (shaped(leaf_pos), shaped(source_pos), shaped(source_force)))
    return result.reshape(leaf_pos.shape)

def unpermute(values, order_rows):

    def one_device(value_block, order_block):
        return jnp.zeros_like(value_block).at[:, order_block].set(value_block)
    return jax.vmap(one_device, in_axes=(1, 0), out_axes=1)(values, order_rows)

def group_shift(leaf_array, direction):
    shaped = leaf_array.reshape((N_GRP, -1) + leaf_array.shape[1:])
    zero_leaf = jnp.zeros_like(shaped[:, :1])
    if direction < 0:
        moved = jnp.concatenate([zero_leaf, shaped[:, :-1]], axis=1)
    else:
        moved = jnp.concatenate([shaped[:, 1:], zero_leaf], axis=1)
    return moved.reshape(leaf_array.shape)

def route_to_leaves(node_values, send_order, leaf_order):
    all_devices = N_GRP * N_TILE
    share = NODE_DEV // N_TILE
    shaped = node_values.reshape(3, all_devices, NODE_DEV)
    sent = jnp.take_along_axis(shaped, send_order[None], axis=2)
    received = sent.reshape(3, N_GRP, N_TILE, N_TILE, share).transpose(0, 1, 3, 2, 4).reshape(3, all_devices, NODE_DEV)
    in_leaves = jnp.take_along_axis(received, leaf_order[None], axis=2)
    return in_leaves.reshape(3, LEAVES, LEAF_PTS).transpose(1, 0, 2)

def route_back(leaf_values, send_order, leaf_order):
    all_devices = N_GRP * N_TILE
    share = NODE_DEV // N_TILE
    flat = leaf_values.transpose(1, 0, 2).reshape(3, all_devices, NODE_DEV)
    in_slots = unpermute(flat, leaf_order)
    returned = in_slots.reshape(3, N_GRP, N_TILE, N_TILE, share).transpose(0, 1, 3, 2, 4).reshape(3, all_devices, NODE_DEV)
    return unpermute(returned, send_order).reshape(3, NODES)

def apply_operator(fiber_vec, nucleus_vec, fiber_ops, body_op, leaf_pos, send_order, leaf_order, leaf_masks, nucleus_rows, nucleus_cols):
    all_devices = N_GRP * N_TILE
    fiber_bf = fiber_vec.astype(jnp.bfloat16)
    nucleus_bf = nucleus_vec.astype(jnp.bfloat16)

    def per_device(pieces):
        return jnp.einsum('fij,fj->fi', pieces[0].astype(jnp.float32), pieces[1].astype(jnp.float32))
    fiber_prod = lax.map(per_device, (fiber_ops.reshape(all_devices, FIB_DEV, ORDER, ORDER), fiber_bf.reshape(all_devices, FIB_DEV, ORDER)))
    fiber_out = fiber_vec + fiber_prod.reshape(FIBERS, ORDER)
    nucleus_out = nucleus_vec + jnp.dot(nucleus_bf.astype(jnp.float32), body_op.T.astype(jnp.float32), preferred_element_type=jnp.float32)
    end_cols = jnp.arange(3) * FNODES
    fiber_out = fiber_out.at[:, end_cols].add(-kappa_coef * nucleus_bf[nucleus_rows[:, None], nucleus_cols].astype(jnp.float32))
    nucleus_out = nucleus_out.at[nucleus_rows[:, None], nucleus_cols].add(-kappa_coef * fiber_vec[:, end_cols])
    forces = fiber_vec[:, :3 * FNODES].reshape(FIBERS, 3, FNODES).transpose(1, 0, 2).reshape(3, NODES)
    leaf_force = route_to_leaves(forces, send_order, leaf_order)
    block_size = math.gcd(LEAVES, 64)
    velocity = window_velocity(leaf_pos, group_shift(leaf_pos, -1), group_shift(leaf_pos, 1), leaf_force, group_shift(leaf_force, -1), group_shift(leaf_force, 1), leaf_masks, block_size)
    node_vel = route_back(velocity, send_order, leaf_order)
    hydro_term = node_vel.reshape(3, FIBERS, FNODES).transpose(1, 0, 2).reshape(FIBERS, 3 * FNODES)
    fiber_out = fiber_out + jnp.concatenate([hydro_term, jnp.zeros((FIBERS, FNODES), jnp.float32)], axis=1)
    return (fiber_out, nucleus_out)

def inner_product(first, second):
    return jnp.sum(first[0] * second[0]) + jnp.sum(first[1] * second[1])

def reference(rhs_fiber, rhs_body, fiber_ops, body_op, positions, send_order, leaf_order, neighbours, attach_nucleus, attach_node):
    leaf_pos = route_to_leaves(positions, send_order, leaf_order)
    leaf_masks = neighbours.astype(jnp.float32)
    fiber_group = jnp.arange(FIBERS, dtype=jnp.int32) // (FIB_DEV * N_TILE)
    nucleus_rows = fiber_group * NUC_GRP + attach_nucleus
    nucleus_cols = (jnp.arange(3, dtype=jnp.int32) * BNODES)[None, :] + attach_node[:, None]
    start_norm = jnp.sqrt(inner_product((rhs_fiber, rhs_body), (rhs_fiber, rhs_body)))
    basis = [(rhs_fiber / start_norm, rhs_body / start_norm)]
    hessen = jnp.zeros((ITERS + 1, ITERS), jnp.float32)
    for j in range(ITERS):
        image = apply_operator(basis[j][0], basis[j][1], fiber_ops, body_op, leaf_pos, send_order, leaf_order, leaf_masks, nucleus_rows, nucleus_cols)
        coeffs = [inner_product(image, vector) for vector in basis]
        fiber_w, nucleus_w = image
        for i in range(j + 1):
            fiber_w = fiber_w - coeffs[i] * basis[i][0]
            nucleus_w = nucleus_w - coeffs[i] * basis[i][1]
        new_length = jnp.sqrt(inner_product((fiber_w, nucleus_w), (fiber_w, nucleus_w)))
        for i in range(j + 1):
            hessen = hessen.at[i, j].set(coeffs[i])
        hessen = hessen.at[j + 1, j].set(new_length)
        if j + 1 < ITERS:
            basis.append((fiber_w / new_length, nucleus_w / new_length))
    gram = jnp.dot(hessen.T, hessen, precision=lax.Precision.HIGHEST)
    target = start_norm * hessen[0, :]
    factor = jnp.linalg.cholesky(gram)
    weights = jax.scipy.linalg.cho_solve((factor, True), target)
    sol_fiber = jnp.zeros_like(rhs_fiber)
    sol_body = jnp.zeros_like(rhs_body)
    for j in range(ITERS):
        sol_fiber = sol_fiber + weights[j] * basis[j][0]
        sol_body = sol_body + weights[j] * basis[j][1]
    return (sol_fiber, sol_body)
```

```python
import functools
import math

import jax
import jax.numpy as jnp
from jax import lax
from jax.experimental import pallas as pl
from jax.experimental.pallas import tpu as pltpu
from jax.sharding import PartitionSpec as P

FNODES = 64
BNODES = 1536
LEAF_PTS = 128
ITERS = 3

kappa_coef = 0.5
eps_square = 0.0025
stokes_coef = 1.0 / (16.0 * math.pi)

F32 = jnp.float32
BF16 = jnp.bfloat16
VMEM_LIMIT = 48 * 1024 * 1024


def iota(shape, dim):
    return lax.broadcasted_iota(jnp.int32, shape, dim)


def split2(x):
    hi = x.astype(BF16)
    return hi, (x - hi.astype(F32)).astype(BF16)


def gather_rows(halves, idx_ref, rows_ref, add):
    rows = halves[0].shape[0]
    lane = iota((rows, 128), 1)
    parts = []
    for c in range(3):
        keep = (lane < 64) if c % 2 == 0 else (lane >= 64)
        hi, low = split2(jnp.where(keep, halves[c // 2], 0.0))
        parts.append(jnp.concatenate([hi, low], axis=1))
    lhs = jnp.concatenate(parts, axis=0)
    blocks = idx_ref.shape[0]
    per = 4
    for b in range(0, blocks, per):
        idx = jnp.concatenate([idx_ref[b + k : b + k + 1, :] for k in range(per)], axis=1)
        hi_idx = idx >> 6
        lo_idx = idx & 63
        one = jnp.where(iota((64, per * 128), 0) == lo_idx, 1.0, 0.0).astype(BF16)
        table = jnp.concatenate([one] * 4, axis=0)
        picked = jnp.dot(lhs, table, preferred_element_type=F32)
        mask = iota((rows, per * 128), 0) == hi_idx
        for c in range(3):
            row = jnp.sum(
                jnp.where(mask, picked[c * rows : (c + 1) * rows], 0.0), axis=0, keepdims=True
            )
            for k in range(per):
                piece = row[:, k * 128 : (k + 1) * 128]
                if add:
                    rows_ref[c, b + k : b + k + 1, :] += piece
                else:
                    rows_ref[c, b + k : b + k + 1, :] = piece


def rows_to_halves(rows_ref, first_ref, second_ref):
    x0, x1, x2 = rows_ref[0], rows_ref[1], rows_ref[2]
    n = x0.shape[0]
    low = iota(x0.shape, 1) < 64
    first_ref[pl.ds(0, n, stride=2), :] = jnp.where(low, x0, pltpu.roll(x1, 64, 1))
    first_ref[pl.ds(1, n, stride=2), :] = jnp.where(low, pltpu.roll(x0, 64, 1), x1)
    second_ref[pl.ds(0, n, stride=2), :] = jnp.where(low, x2, 0.0)
    second_ref[pl.ds(1, n, stride=2), :] = jnp.where(low, pltpu.roll(x2, 64, 1), 0.0)


def halves_to_rows(first_ref, second_ref, rows_ref):
    n = rows_ref.shape[1]
    low = iota((n, 128), 1) < 64
    h0 = first_ref[pl.ds(0, n, stride=2), :]
    h1 = first_ref[pl.ds(1, n, stride=2), :]
    g0 = second_ref[pl.ds(0, n, stride=2), :]
    g1 = second_ref[pl.ds(1, n, stride=2), :]
    rows_ref[0] = jnp.where(low, h0, pltpu.roll(h1, 64, 1))
    rows_ref[1] = jnp.where(low, pltpu.roll(h0, 64, 1), h1)
    rows_ref[2] = jnp.where(low, g0, pltpu.roll(g1, 64, 1))


def scatter_halves(rows_ref, idx_ref, rows):
    blocks = idx_ref.shape[0]
    total = jnp.zeros((6 * rows, 128), F32)
    for b in range(0, blocks, 2):
        idx = jnp.concatenate([idx_ref[b : b + 1, :], idx_ref[b + 1 : b + 2, :]], axis=1)
        hi_idx = idx >> 6
        lo_idx = idx & 63
        one = jnp.where(iota((128, 256), 0) == lo_idx, 1.0, 0.0).astype(BF16)
        mask = jnp.where(iota((rows, 256), 0) == hi_idx, 1.0, 0.0)
        his, lows = [], []
        for c in range(3):
            x = jnp.concatenate(
                [rows_ref[c, b : b + 1, :], rows_ref[c, b + 1 : b + 2, :]], axis=1
            )
            hi, low = split2(x)
            his.append((mask * hi.astype(F32)).astype(BF16))
            lows.append((mask * low.astype(F32)).astype(BF16))
        lhs = jnp.concatenate(his + lows, axis=0)
        total += lax.dot_general(
            lhs, one, (((1,), (1,)), ((), ())), preferred_element_type=F32
        )
    parts = [
        total[c * rows : (c + 1) * rows] + total[(3 + c) * rows : (4 + c) * rows]
        for c in range(3)
    ]
    return parts[0] + pltpu.roll(parts[1], 64, 1), parts[2]


def send_kernel(exact, x_ref, idx_ref, out_ref, rows_ref, first_ref, second_ref):
    halves = (x_ref[:, :128], x_ref[:, 128:])
    gather_rows(halves, idx_ref, rows_ref, False)
    if exact:
        rest = []
        for x in halves:
            hi, low = split2(x)
            rest.append(x - hi.astype(F32) - low.astype(F32))
        gather_rows(rest, idx_ref, rows_ref, True)
    rows_to_halves(rows_ref, first_ref, second_ref)
    out_ref[:, :128] = first_ref[...]
    out_ref[:, 128:] = second_ref[...]


def leaf_kernel(exact, x_ref, idx_ref, out_ref):
    halves = (x_ref[:, :128], x_ref[:, 128:])
    gather_rows(halves, idx_ref, out_ref, False)
    if exact:
        rest = []
        for x in halves:
            hi, low = split2(x)
            rest.append(x - hi.astype(F32) - low.astype(F32))
        gather_rows(rest, idx_ref, out_ref, True)


def stokes_kernel(src_ref, near_ref, idx_ref, out_ref, acc_ref, rows_ref):
    leaves = src_ref.shape[0] - 2
    acc_ref[...] = jnp.zeros_like(acc_ref)

    def one_source(m, carry):
        tile = src_ref[m]
        cols = jnp.transpose(tile)
        near = [near_ref[m, 0], None, near_ref[m, 1]]
        targets = []
        for d in range(3):
            t = jnp.clip(m + d - 1, 0, leaves + 1)
            targets.append([src_ref[t, c : c + 1, :] for c in range(3)])
        sums = [[jnp.zeros((8, 128), F32) for _ in range(3)] for _ in range(3)]
        for s in range(LEAF_PTS // 8):
            col = [
                jnp.broadcast_to(cols[s * 8 : (s + 1) * 8, c : c + 1], (8, 128)) for c in range(6)
            ]
            for d in range(3):
                dx = targets[d][0] - col[0]
                dy = targets[d][1] - col[1]
                dz = targets[d][2] - col[2]
                r2 = dx * dx + dy * dy + dz * dz
                along = dx * col[3] + dy * col[4] + dz * col[5]
                r2e = r2 + eps_square
                inv = lax.rsqrt(r2e)
                cube = inv * inv * inv
                direct = (r2e + eps_square) * cube
                scaled = along * cube
                sums[d][0] += direct * col[3] + scaled * dx
                sums[d][1] += direct * col[4] + scaled * dy
                sums[d][2] += direct * col[5] + scaled * dz
        for d in range(3):
            for c in range(3):
                u = sums[d][c]
                if near[d] is not None:
                    u = u * near[d]
                acc_ref[c, m + d] += u
        return carry

    lax.fori_loop(0, leaves + 2, one_source, 0)
    for c in range(3):
        rows_ref[c] = stokes_coef * jnp.sum(acc_ref[c, 2 : leaves + 2], axis=1)
    first, second = scatter_halves(rows_ref, idx_ref, out_ref.shape[0])
    out_ref[:, :128] = first
    out_ref[:, 128:] = second


def back_kernel(x_ref, idx_ref, out_ref, first_ref, second_ref, rows_ref):
    first_ref[...] = x_ref[:, :128]
    second_ref[...] = x_ref[:, 128:]
    halves_to_rows(first_ref, second_ref, rows_ref)
    first, second = scatter_halves(rows_ref, idx_ref, out_ref.shape[0])
    out_ref[:, :128] = first
    out_ref[:, 128:] = second


def call(kernel, out, scratch, smem=(), count=2):
    specs = [
        pl.BlockSpec(memory_space=pltpu.SMEM if i in smem else pltpu.VMEM) for i in range(count)
    ]
    return pl.pallas_call(
        kernel,
        out_shape=jax.ShapeDtypeStruct(out, F32),
        in_specs=specs,
        out_specs=pl.BlockSpec(memory_space=pltpu.VMEM),
        scratch_shapes=[pltpu.VMEM(s, F32) for s in scratch],
        compiler_params=pltpu.CompilerParams(vmem_limit_bytes=VMEM_LIMIT),
    )


def inner_product(first, second):
    return jnp.sum(first[0] * second[0]) + jnp.sum(first[1] * second[1])


def shift_ends(array, axis):
    devices = lax.axis_size(axis)
    up = [(i, i + 1) for i in range(devices - 1)]
    down = [(i + 1, i) for i in range(devices - 1)]
    return lax.ppermute(array[-1:], axis, up), lax.ppermute(array[:1], axis, down)


def local(
    rhs_fiber,
    rhs_body,
    fiber_ops,
    body_op,
    positions,
    send_order,
    leaf_order,
    neighbours,
    attach_nucleus,
    attach_node,
):
    tiles = lax.axis_size("tile")
    me = lax.axis_index("tile")
    node_count = positions.shape[1]
    blocks = node_count // 128
    leaves = node_count // LEAF_PTS
    fiber_count, order = rhs_fiber.shape
    nucleus_count, body_cols = rhs_body.shape
    rows = node_count // 64
    chunk = rows // tiles
    send_index = send_order.reshape(blocks, 128)
    leaf_index = leaf_order.reshape(blocks, 128)
    nb = neighbours.astype(F32)
    zero = jnp.zeros((1,), F32)
    near = jnp.stack(
        [
            jnp.concatenate([zero, zero, nb[:, 1]]),
            jnp.concatenate([nb[:, 0], zero, zero]),
        ],
        axis=1,
    )

    def send(exact):
        return call(
            functools.partial(send_kernel, exact),
            (rows, 256),
            [(3, blocks, 128), (rows, 128), (rows, 128)],
        )

    def to_leaf(exact):
        return call(functools.partial(leaf_kernel, exact), (3, blocks, 128), [])

    stokes = call(
        stokes_kernel,
        (rows, 256),
        [(3, leaves + 4, 8, 128), (3, blocks, 128)],
        smem=(1,),
        count=3,
    )
    back = call(back_kernel, (rows, 256), [(rows, 128), (rows, 128), (3, blocks, 128)])

    pos_nodes = positions.reshape(3, rows, 64).transpose(1, 0, 2).reshape(rows, 192)
    pos_nodes = jnp.concatenate([pos_nodes, jnp.zeros((rows, 64), F32)], axis=1)
    pos_sent = send(True)(pos_nodes, send_index)
    pos_recv = lax.all_to_all(pos_sent, "tile", split_axis=0, concat_axis=0, tiled=True)
    leaf_pos = to_leaf(True)(pos_recv, leaf_index).transpose(1, 0, 2)
    pos_left, pos_right = shift_ends(leaf_pos, "tile")
    pos_rim = jnp.concatenate([pos_left, leaf_pos, pos_right], axis=0)
    pad = jnp.zeros((leaves + 2, 2, 128), F32)

    group_attach = lax.all_gather(
        jnp.stack([attach_nucleus, attach_node]).astype(F32), "tile", axis=1, tiled=True
    ).astype(jnp.int32)
    group_nucleus, group_node = group_attach[0], group_attach[1]
    comp = jnp.arange(3, dtype=jnp.int32) * BNODES
    my_cols = me * body_cols + jnp.arange(body_cols, dtype=jnp.int32)
    nucleus_pick = (
        jnp.arange(nucleus_count, dtype=jnp.int32)[:, None] == group_nucleus[None, :]
    )
    col_pick = (
        (comp[:, None] + group_node[None, :]).reshape(-1)[:, None] == my_cols[None, :]
    ).astype(BF16)
    nucleus_pick3 = jnp.concatenate([nucleus_pick] * 3, axis=1)
    own_pick = (
        attach_nucleus[:, None] == jnp.arange(nucleus_count, dtype=jnp.int32)[None, :]
    ).astype(BF16)
    own_cols = attach_node[:, None] == jnp.arange(BNODES, dtype=jnp.int32)[None, :]

    start_norm = jnp.sqrt(
        lax.psum(inner_product((rhs_fiber, rhs_body), (rhs_fiber, rhs_body)), ("grp", "tile"))
    )
    basis = [(rhs_fiber / start_norm, rhs_body / start_norm)]
    hessen = jnp.zeros((ITERS + 1, ITERS), F32)
    for j in range(ITERS):
        fiber_vec, nucleus_vec = basis[j]
        fiber_bf = fiber_vec.astype(BF16)
        nucleus_bf = nucleus_vec.astype(BF16)
        nucleus_full = lax.all_gather(nucleus_bf, "tile", axis=1, tiled=True)
        sent = send(False)(fiber_vec, send_index).reshape(tiles, chunk, 256)
        ends = fiber_vec.reshape(fiber_count, order // FNODES, FNODES)[:, :3, 0]
        ends_row = jnp.concatenate(
            [ends.T.reshape(1, 1, 3 * fiber_count), jnp.zeros((1, 1, 256 - 3 * fiber_count), F32)],
            axis=2,
        )
        sent = jnp.concatenate([sent, jnp.broadcast_to(ends_row, (tiles, 1, 256))], axis=1)
        recv = lax.all_to_all(sent, "tile", split_axis=0, concat_axis=0, tiled=True)
        leaf_force = to_leaf(False)(recv[:, :chunk].reshape(rows, 256), leaf_index).transpose(
            1, 0, 2
        )
        left, right = shift_ends(leaf_force.astype(BF16), "tile")
        force_rim = jnp.concatenate([left.astype(F32), leaf_force, right.astype(F32)], axis=0)
        sources = jnp.concatenate([pos_rim, force_rim, pad], axis=1)
        slots = stokes(sources, near, leaf_index)
        returned = lax.all_to_all(slots, "tile", split_axis=0, concat_axis=0, tiled=True)
        hydro = back(returned, send_index)

        fiber_out = fiber_vec + jnp.einsum(
            "fij,fj->fi", fiber_ops, fiber_bf, preferred_element_type=F32
        )
        nucleus_out = nucleus_vec + lax.dot_general(
            nucleus_full, body_op, (((1,), (1,)), ((), ())), preferred_element_type=F32
        )
        at_nucleus = jnp.dot(own_pick, nucleus_full, preferred_element_type=F32).reshape(
            fiber_count, 3, BNODES
        )
        felt = jnp.sum(jnp.where(own_cols[:, None, :], at_nucleus, 0.0), axis=2)
        felt_full = jnp.pad(felt[:, :, None], ((0, 0), (0, 1), (0, FNODES - 1))).reshape(
            fiber_count, order
        )
        fiber_out = fiber_out - kappa_coef * felt_full + hydro
        all_ends = (
            recv[:, chunk, : 3 * fiber_count]
            .reshape(tiles, 3, fiber_count)
            .transpose(1, 0, 2)
            .reshape(1, -1)
        )
        ends_hi, ends_low = split2(all_ends)
        pulled = jnp.dot(
            jnp.where(nucleus_pick3, ends_hi, 0), col_pick, preferred_element_type=F32
        ) + jnp.dot(jnp.where(nucleus_pick3, ends_low, 0), col_pick, preferred_element_type=F32)
        nucleus_out = nucleus_out - kappa_coef * pulled

        image = (fiber_out, nucleus_out)
        local_dots = [inner_product(image, vector) for vector in basis]
        merged = lax.psum(jnp.stack(local_dots + [inner_product(image, image)]), ("grp", "tile"))
        coeffs = merged[:-1]
        fiber_w, nucleus_w = image
        for i in range(j + 1):
            fiber_w = fiber_w - coeffs[i] * basis[i][0]
            nucleus_w = nucleus_w - coeffs[i] * basis[i][1]
        new_length = jnp.sqrt(merged[-1] - jnp.sum(coeffs * coeffs))
        for i in range(j + 1):
            hessen = hessen.at[i, j].set(coeffs[i])
        hessen = hessen.at[j + 1, j].set(new_length)
        if j + 1 < ITERS:
            basis.append((fiber_w / new_length, nucleus_w / new_length))
    gram = jnp.dot(hessen.T, hessen, precision=lax.Precision.HIGHEST)
    target = start_norm * hessen[0, :]
    factor = jnp.linalg.cholesky(gram)
    weights = jax.scipy.linalg.cho_solve((factor, True), target)
    sol_fiber = jnp.zeros_like(rhs_fiber)
    sol_body = jnp.zeros_like(rhs_body)
    for j in range(ITERS):
        sol_fiber = sol_fiber + weights[j] * basis[j][0]
        sol_body = sol_body + weights[j] * basis[j][1]
    return (sol_fiber, sol_body)


def solution(mesh):
    placed = (
        P(("grp", "tile"), None),
        P("grp", "tile"),
        P(("grp", "tile"), None, None),
        P("tile", None),
        P(None, ("grp", "tile")),
        P(("grp", "tile"), None),
        P(("grp", "tile"), None),
        P(("grp", "tile"), None),
        P(("grp", "tile")),
        P(("grp", "tile")),
    )
    return jax.shard_map(
        local,
        mesh=mesh,
        in_specs=placed,
        out_specs=(P(("grp", "tile"), None), P("grp", "tile")),
        check_vma=False,
    )
```

```python
import functools
import math

import jax
import jax.numpy as jnp
from jax import lax
from jax.experimental import pallas as pl
from jax.experimental.pallas import tpu as pltpu
from jax.sharding import PartitionSpec as P

FNODES = 64
BNODES = 1536
LEAF_PTS = 128
ITERS = 3

kappa_coef = 0.5
eps_square = 0.0025
stokes_coef = 1.0 / (16.0 * math.pi)

F32 = jnp.float32
BF16 = jnp.bfloat16
VMEM_LIMIT = 48 * 1024 * 1024


def iota(shape, dim):
    return lax.broadcasted_iota(jnp.int32, shape, dim)


def split2(x):
    hi = x.astype(BF16)
    return hi, (x - hi.astype(F32)).astype(BF16)


def gather_rows(halves, idx_ref, store):
    rows = halves[0].shape[0]
    lane = iota((rows, 128), 1)
    parts = []
    for c in range(3):
        keep = (lane < 64) if c % 2 == 0 else (lane >= 64)
        hi, low = split2(jnp.where(keep, halves[c // 2], 0.0))
        parts.append(jnp.concatenate([hi, low], axis=1))
    lhs = jnp.concatenate(parts, axis=0)
    blocks = idx_ref.shape[0]
    per = 4
    for b in range(0, blocks, per):
        idx = jnp.concatenate([idx_ref[b + k : b + k + 1, :] for k in range(per)], axis=1)
        hi_idx = idx >> 6
        lo_idx = idx & 63
        one = jnp.where(iota((64, per * 128), 0) == lo_idx, 1.0, 0.0).astype(BF16)
        table = jnp.concatenate([one] * 4, axis=0)
        picked = jnp.dot(lhs, table, preferred_element_type=F32)
        mask = iota((rows, per * 128), 0) == hi_idx
        for c in range(3):
            row = jnp.sum(
                jnp.where(mask, picked[c * rows : (c + 1) * rows], 0.0), axis=0, keepdims=True
            )
            for k in range(per):
                store(c, b + k, row[:, k * 128 : (k + 1) * 128])


def gather_exact(halves, idx_ref, store, add):
    gather_rows(halves, idx_ref, store)
    rest = []
    for x in halves:
        hi, low = split2(x)
        rest.append(x - hi.astype(F32) - low.astype(F32))
    gather_rows(rest, idx_ref, add)


def rows_to_halves(rows_ref, first_ref, second_ref):
    x0, x1, x2 = rows_ref[0], rows_ref[1], rows_ref[2]
    n = x0.shape[0]
    low = iota(x0.shape, 1) < 64
    first_ref[pl.ds(0, n, stride=2), :] = jnp.where(low, x0, pltpu.roll(x1, 64, 1))
    first_ref[pl.ds(1, n, stride=2), :] = jnp.where(low, pltpu.roll(x0, 64, 1), x1)
    second_ref[pl.ds(0, n, stride=2), :] = jnp.where(low, x2, 0.0)
    second_ref[pl.ds(1, n, stride=2), :] = jnp.where(low, pltpu.roll(x2, 64, 1), 0.0)


def halves_to_rows(first_ref, second_ref, rows_ref):
    n = rows_ref.shape[1]
    low = iota((n, 128), 1) < 64
    h0 = first_ref[pl.ds(0, n, stride=2), :]
    h1 = first_ref[pl.ds(1, n, stride=2), :]
    g0 = second_ref[pl.ds(0, n, stride=2), :]
    g1 = second_ref[pl.ds(1, n, stride=2), :]
    rows_ref[0] = jnp.where(low, h0, pltpu.roll(h1, 64, 1))
    rows_ref[1] = jnp.where(low, pltpu.roll(h0, 64, 1), h1)
    rows_ref[2] = jnp.where(low, g0, pltpu.roll(g1, 64, 1))


def scatter_halves(rows_ref, idx_ref, rows):
    blocks = idx_ref.shape[0]
    total = jnp.zeros((6 * rows, 128), F32)
    for b in range(0, blocks, 2):
        idx = jnp.concatenate([idx_ref[b : b + 1, :], idx_ref[b + 1 : b + 2, :]], axis=1)
        hi_idx = idx >> 6
        lo_idx = idx & 63
        one = jnp.where(iota((128, 256), 0) == lo_idx, 1.0, 0.0).astype(BF16)
        mask = jnp.where(iota((rows, 256), 0) == hi_idx, 1.0, 0.0)
        his, lows = [], []
        for c in range(3):
            x = jnp.concatenate(
                [rows_ref[c, b : b + 1, :], rows_ref[c, b + 1 : b + 2, :]], axis=1
            )
            hi, low = split2(x)
            his.append((mask * hi.astype(F32)).astype(BF16))
            lows.append((mask * low.astype(F32)).astype(BF16))
        lhs = jnp.concatenate(his + lows, axis=0)
        total += lax.dot_general(
            lhs, one, (((1,), (1,)), ((), ())), preferred_element_type=F32
        )
    parts = [
        total[c * rows : (c + 1) * rows] + total[(3 + c) * rows : (4 + c) * rows]
        for c in range(3)
    ]
    return parts[0] + pltpu.roll(parts[1], 64, 1), parts[2]


def total_of(x):
    return jnp.sum(jnp.sum(x, axis=0, keepdims=True), axis=1, keepdims=True)


def nt_dot(a, b):
    return lax.dot_general(a, b, (((1,), (1,)), ((), ())), preferred_element_type=F32)


def one_source(src_ref, near_ref, acc_ref, m):
    count = src_ref.shape[0]
    cols = jnp.transpose(src_ref[m])
    targets = []
    for d in range(3):
        t = (m + d - 1 + count) % count
        targets.append([src_ref[t, c : c + 1, :] for c in range(3)])
    sums = [[jnp.zeros((8, 128), F32) for _ in range(3)] for _ in range(3)]
    for s in range(LEAF_PTS // 8):
        col = [jnp.broadcast_to(cols[s * 8 : (s + 1) * 8, c : c + 1], (8, 128)) for c in range(6)]
        for d in range(3):
            dx = targets[d][0] - col[0]
            dy = targets[d][1] - col[1]
            dz = targets[d][2] - col[2]
            r2e = dx * dx + dy * dy + dz * dz + eps_square
            along = dx * col[3] + dy * col[4] + dz * col[5]
            inv = lax.rsqrt(r2e)
            cube = inv * inv * inv
            direct = (r2e + eps_square) * cube
            scaled = along * cube
            sums[d][0] += direct * col[3] + scaled * dx
            sums[d][1] += direct * col[4] + scaled * dy
            sums[d][2] += direct * col[5] + scaled * dz
    for d in range(3):
        for c in range(3):
            u = sums[d][c]
            if d != 1:
                u = u * near_ref[m, d // 2 : d // 2 + 1, :]
            acc_ref[c, m + d] += u


def whole_kernel(
    tiles,
    grps,
    rhs_f,
    rhs_b,
    ops_hbm,
    body_hbm,
    pos_ref,
    send_idx,
    leaf_idx,
    near_ref,
    meta_ref,
    own_ref,
    sol_f,
    sol_b,
    ops,
    body,
    sbuf,
    rbuf,
    pbuf,
    bs,
    br,
    rows_ref,
    first_ref,
    second_ref,
    src_ref,
    acc_ref,
    full,
    pick,
    colpick,
    vf,
    vb,
    wf,
    wb,
    hs,
    ar1,
    ar2,
    local_sem,
    pos_s,
    pos_r,
    fwd_s,
    fwd_r,
    back_s,
    back_r,
    ag_s,
    ag_r,
    sib_s,
    sib_r,
    rim_s,
    rim_r,
    ar1_s,
    ar1_r,
    ar2_s,
    ar2_r,
):
    me = lax.axis_index("tile")
    grp = lax.axis_index("grp")
    rows = first_ref.shape[0]
    chunk = rows // tiles
    blocks = rows_ref.shape[1]
    leaves = blocks
    nuclei, cols = rhs_b.shape
    npad = full.shape[1]
    fibers, order = rhs_f.shape
    mesh_id = pl.DeviceIdType.MESH

    load_ops = pltpu.make_async_copy(ops_hbm, ops, local_sem.at[0])
    load_body = pltpu.make_async_copy(body_hbm, body, local_sem.at[1])
    load_ops.start()
    load_body.start()

    barrier = pltpu.get_barrier_semaphore()
    for d in range(1, tiles):
        pl.semaphore_signal(
            barrier, inc=1, device_id=(grp, lax.rem(me + d, tiles)), device_id_type=mesh_id
        )
    for d in range(1, grps):
        pl.semaphore_signal(
            barrier, inc=1, device_id=(lax.rem(grp + d, grps), me), device_id_type=mesh_id
        )

    def to_tile(source, target, send_sem, recv_sem, peer):
        return pltpu.make_async_remote_copy(
            src_ref=source,
            dst_ref=target,
            send_sem=send_sem,
            recv_sem=recv_sem,
            device_id=(grp, peer),
            device_id_type=mesh_id,
        )

    def exchange(send, recv, send_sem, recv_sem):
        copies = []
        for d in range(1, tiles):
            peer = lax.rem(me + d, tiles)
            copies.append(
                to_tile(send.at[peer], recv.at[me], send_sem.at[d], recv_sem.at[d], peer)
            )
        return copies

    def reduce_start(p, value):
        ar1[p, me] = value
        copies = []
        for d in range(1, tiles):
            peer = lax.rem(me + d, tiles)
            copies.append(
                to_tile(ar1.at[p, me], ar1.at[p, me], ar1_s.at[p, d], ar1_r.at[p, d], peer)
            )
        for copy in copies:
            copy.start()
        return copies

    def reduce_end(p, copies):
        for copy in copies:
            copy.wait_recv()
        part = ar1[p, 0]
        for t in range(1, tiles):
            part = part + ar1[p, t]
        ar2[p, grp] = part
        second = []
        for d in range(1, grps):
            second.append(
                pltpu.make_async_remote_copy(
                    src_ref=ar2.at[p, grp],
                    dst_ref=ar2.at[p, grp],
                    send_sem=ar2_s.at[p, d],
                    recv_sem=ar2_r.at[p, d],
                    device_id=(lax.rem(grp + d, grps), me),
                    device_id_type=mesh_id,
                )
            )
        for copy in second:
            copy.start()
        for copy in second:
            copy.wait_recv()
        total = ar2[p, 0]
        for g in range(1, grps):
            total = total + ar2[p, g]
        for copy in copies + second:
            copy.wait_send()
        return total

    def keep_rows(c, b, piece):
        rows_ref[c, b : b + 1, :] = piece

    def add_rows(c, b, piece):
        rows_ref[c, b : b + 1, :] += piece

    def fill_send(extra, own_buf):
        rows_to_halves(rows_ref, first_ref, second_ref)
        for t in range(tiles):
            sbuf[t, 0:chunk, 0:128] = first_ref[t * chunk : (t + 1) * chunk, :]
            sbuf[t, 0:chunk, 128:256] = second_ref[t * chunk : (t + 1) * chunk, :]
            sbuf[t, 8:16, :] = extra
        own_buf[me] = sbuf[me]

    def received(buf):
        for t in range(tiles):
            first_ref[t * chunk : (t + 1) * chunk, :] = buf[t, 0:chunk, 0:128]
            second_ref[t * chunk : (t + 1) * chunk, :] = buf[t, 0:chunk, 128:256]

    gather_exact((pos_ref[:, :128], pos_ref[:, 128:]), send_idx, keep_rows, add_rows)
    fill_send(meta_ref[...], pbuf)
    pl.semaphore_wait(barrier, tiles + grps - 2)
    copies = exchange(sbuf, pbuf, pos_s, pos_r)
    for copy in copies:
        copy.start()
    norm = total_of(rhs_f[...] * rhs_f[...]) + total_of(rhs_b[...] * rhs_b[...])
    sums = reduce_start(0, jnp.broadcast_to(norm, (8, 128)))
    vf[...] = jnp.zeros_like(vf)
    vb[...] = jnp.zeros_like(vb)
    src_ref[...] = jnp.zeros_like(src_ref)
    for copy in copies:
        copy.wait_recv()
    received(pbuf)

    def keep_pos(c, b, piece):
        src_ref[1 + b, c : c + 1, :] = piece

    def add_pos(c, b, piece):
        src_ref[1 + b, c : c + 1, :] += piece

    gather_exact((first_ref[...], second_ref[...]), leaf_idx, keep_pos, add_pos)
    for t in range(tiles):
        nuc_row = pbuf[t, 8:9, :]
        col_row = pbuf[t, 9:10, :]
        pick[t] = jnp.where(iota((npad, 256), 0).astype(F32) == nuc_row, 1.0, 0.0).astype(BF16)
        my_col = (iota((cols, 256), 0) + me * cols).astype(F32)
        colpick[t] = jnp.where(my_col == col_row, 1.0, 0.0).astype(BF16)
    for copy in copies:
        copy.wait_send()
    beta = jnp.sqrt(reduce_end(0, sums))[0:1]
    beta1 = beta[:, 0:1]
    vf[0] = rhs_f[...] / beta1
    vb[0, 0:nuclei, :] = rhs_b[...] / beta1
    load_ops.wait()
    load_body.wait()

    def step(j, carry):
        p = (j + 1) % 2
        fiber = vf[j]
        full[me] = vb[j].astype(BF16)
        gather_rows((fiber[:, :128], fiber[:, 128:]), send_idx, keep_rows)
        end_pick = jnp.where(iota((8, order), 1) == iota((8, order), 0) * FNODES, 1.0, 0.0)
        end_pick = jnp.where(iota((8, order), 0) < 3, end_pick, 0.0).astype(BF16)
        hi, low = split2(fiber)
        ends = nt_dot(end_pick, hi) + nt_dot(end_pick, low)
        ends = jnp.concatenate([ends, jnp.zeros((8, 128 - fibers), F32)], axis=1)
        ends_row = jnp.concatenate(
            [ends[0:1] + pltpu.roll(ends, 64, 1)[1:2], ends[2:3]], axis=1
        )
        fill_send(jnp.broadcast_to(ends_row, (8, 256)), rbuf)
        forward = exchange(sbuf, rbuf, fwd_s, fwd_r)
        for copy in forward:
            copy.start()

        wide = jnp.concatenate([fiber, jnp.zeros((128 - fibers, order), F32)], axis=0)
        vec_t = jnp.transpose(wide).astype(BF16)

        def one_fiber(f, sofar):
            out = jnp.dot(ops[f], vec_t, preferred_element_type=F32)
            return jnp.where(iota((order, 128), 1) == f, out, sofar)

        prod = lax.fori_loop(0, fibers, one_fiber, jnp.zeros((order, 128), F32))
        wf[...] = fiber + jnp.transpose(prod)[:fibers]

        for copy in forward:
            copy.wait_recv()
        received(rbuf)

        def keep_force(c, b, piece):
            src_ref[1 + b, 3 + c : 4 + c, :] = piece

        gather_rows((first_ref[...], second_ref[...]), leaf_idx, keep_force)
        up = to_tile(
            src_ref.at[leaves], src_ref.at[0], rim_s.at[0], rim_r.at[0], lax.rem(me + 1, tiles)
        )
        down = to_tile(
            src_ref.at[1],
            src_ref.at[leaves + 1],
            rim_s.at[1],
            rim_r.at[1],
            lax.rem(me + tiles - 1, tiles),
        )
        up.start()
        down.start()
        sibling = me + 1 - 2 * (me % 2)
        spread = []
        for d in range(2, tiles, 2):
            peer = lax.rem(me + d, tiles)
            spread.append(to_tile(full.at[me], full.at[me], ag_s.at[d], ag_r.at[d], peer))
        paired = [to_tile(full.at[me], full.at[me], sib_s.at[0], sib_r.at[0], sibling)]
        for copy in spread + paired:
            copy.start()

        acc_ref[...] = jnp.zeros_like(acc_ref)

        def inside(m, c):
            one_source(src_ref, near_ref, acc_ref, m)
            return c

        lax.fori_loop(2, leaves, inside, 0)
        up.wait()
        down.wait()

        def edges(k, c):
            m = k % 2 + (k // 2) * leaves
            one_source(src_ref, near_ref, acc_ref, m)
            return c

        lax.fori_loop(0, 4, edges, 0)
        for c in range(3):
            rows_ref[c] = stokes_coef * jnp.sum(acc_ref[c, 2 : leaves + 2], axis=1)
        first, second = scatter_halves(rows_ref, leaf_idx, rows)
        for t in range(tiles):
            bs[t, 0:chunk, 0:128] = first[t * chunk : (t + 1) * chunk]
            bs[t, 0:chunk, 128:256] = second[t * chunk : (t + 1) * chunk]
        br[me] = bs[me]
        back = exchange(bs, br, back_s, back_r)
        for copy in back:
            copy.start()
        for i, copy in enumerate(spread):
            copy.wait_recv()
            got = lax.rem(me + tiles - 2 * (i + 1), tiles)
            paired.append(
                to_tile(full.at[got], full.at[got], sib_s.at[i + 1], sib_r.at[i + 1], sibling)
            )
            paired[-1].start()

        wb[...] = vb[j]
        for t in range(tiles):
            row = rbuf[t, 8:9, :]
            row_hi, row_low = split2(row)
            where = pick[t].astype(F32)
            lhs = jnp.concatenate(
                [(where * row_hi.astype(F32)).astype(BF16), (where * row_low.astype(F32)).astype(BF16)],
                axis=0,
            )
            pulled = nt_dot(lhs, colpick[t])
            wb[...] -= kappa_coef * (pulled[:npad] + pulled[npad:])
        for copy in paired:
            copy.wait_recv()

        def one_block(t, c):
            wb[...] += nt_dot(full[t], body[t])
            return c

        lax.fori_loop(0, tiles, one_block, 0)
        own_pick = jnp.where(iota((fibers, npad), 1) == own_ref[0, :, :npad], 1.0, 0.0).astype(BF16)
        node = own_ref[1, :, 0:1]
        felt = [jnp.zeros((fibers, 1), F32) for _ in range(3)]
        for t in range(tiles):
            picked = jnp.dot(own_pick, full[t], preferred_element_type=F32)
            at = iota((fibers, cols), 1) + t * cols
            for c in range(3):
                if t * cols < (c + 1) * BNODES and (t + 1) * cols > c * BNODES:
                    felt[c] += jnp.sum(
                        jnp.where(at == node + c * BNODES, picked, 0.0), axis=1, keepdims=True
                    )
        lane = iota((fibers, order), 1)
        for c in range(3):
            wf[...] -= kappa_coef * jnp.where(lane == c * FNODES, felt[c], 0.0)

        for copy in back:
            copy.wait_recv()
        received(br)
        halves_to_rows(first_ref, second_ref, rows_ref)
        first, second = scatter_halves(rows_ref, send_idx, rows)
        wf[:, 0:128] += first
        wf[:, 128:256] += second
        for copy in forward + back + spread + paired:
            copy.wait_send()

        fib, nuc = wf[...], wb[...]
        dots = [total_of(fib * vf[i]) + total_of(nuc * vb[i]) for i in range(3)]
        dots.append(total_of(fib * fib) + total_of(nuc * nuc))
        line = iota((8, 128), 0)
        value = jnp.zeros((8, 128), F32)
        for i in range(4):
            value = jnp.where(line == i, dots[i], value)
        total = reduce_end(p, reduce_start(p, value))
        length = jnp.sqrt(
            total[3:4]
            - (total[0:1] * total[0:1] + total[1:2] * total[1:2] + total[2:3] * total[2:3])
        )
        for i in range(3):
            h = total[i : i + 1, 0:1]
            fib = fib - h * vf[i]
            nuc = nuc - h * vb[i]
        vf[j + 1] = fib / length[:, 0:1]
        vb[j + 1] = nuc / length[:, 0:1]
        hs[j] = jnp.where(line == 3, length, total)
        return carry

    lax.fori_loop(0, ITERS, step, 0)

    h = [[None] * 3 for _ in range(4)]
    for j in range(3):
        for i in range(j + 1):
            h[i][j] = hs[j, i : i + 1, :]
        h[j + 1][j] = hs[j, 3:4, :]
    gram = [[None] * 3 for _ in range(3)]
    for i in range(3):
        for j in range(i + 1):
            value = jnp.zeros((1, 128), F32)
            for k in range(j + 2):
                value = value + h[k][i] * h[k][j]
            gram[i][j] = value
    l00 = jnp.sqrt(gram[0][0])
    l10 = gram[1][0] / l00
    l20 = gram[2][0] / l00
    l11 = jnp.sqrt(gram[1][1] - l10 * l10)
    l21 = (gram[2][1] - l20 * l10) / l11
    l22 = jnp.sqrt(gram[2][2] - l20 * l20 - l21 * l21)
    z0 = beta * h[0][0] / l00
    z1 = (beta * h[0][1] - l10 * z0) / l11
    z2 = (beta * h[0][2] - l20 * z0 - l21 * z1) / l22
    y2 = z2 / l22
    y1 = (z1 - l21 * y2) / l11
    y0 = (z0 - l10 * y1 - l20 * y2) / l00
    y0, y1, y2 = y0[:, 0:1], y1[:, 0:1], y2[:, 0:1]
    sol_f[...] = y0 * vf[0] + y1 * vf[1] + y2 * vf[2]
    body_out = y0 * vb[0] + y1 * vb[1] + y2 * vb[2]
    sol_b[...] = body_out[:nuclei]


def local(
    rhs_fiber,
    rhs_body,
    fiber_ops,
    body_op,
    positions,
    send_order,
    leaf_order,
    neighbours,
    attach_nucleus,
    attach_node,
):
    tiles = lax.axis_size("tile")
    grps = lax.axis_size("grp")
    me = lax.axis_index("tile")
    node_count = positions.shape[1]
    blocks = node_count // 128
    leaves = node_count // LEAF_PTS
    fibers, order = rhs_fiber.shape
    nuclei, cols = rhs_body.shape
    npad = -(-nuclei // 16) * 16
    rows = node_count // 64
    send_index = send_order.reshape(blocks, 128)
    leaf_index = leaf_order.reshape(blocks, 128)
    nb = neighbours.astype(F32)
    zero = jnp.zeros((1,), F32)
    leaf_id = jnp.arange(leaves)
    left = jnp.where((leaf_id == 0) & (me == 0), 0.0, nb[:, 0])
    right = jnp.where((leaf_id == leaves - 1) & (me == tiles - 1), 0.0, nb[:, 1])
    near = jnp.stack(
        [jnp.concatenate([zero, zero, right]), jnp.concatenate([left, zero, zero])]
        + [jnp.zeros((leaves + 2,), F32)] * 6,
        axis=1,
    )
    near = jnp.broadcast_to(near[:, :, None], (leaves + 2, 8, 128))
    pos_nodes = positions.reshape(3, rows, 64).transpose(1, 0, 2).reshape(rows, 192)
    pos_nodes = jnp.concatenate([pos_nodes, jnp.zeros((rows, 64), F32)], axis=1)
    body_blocks = body_op.reshape(cols, tiles, cols).transpose(1, 0, 2)
    comp = jnp.arange(3, dtype=jnp.int32)[:, None] * BNODES
    target = jnp.concatenate(
        [(attach_node[None, :] + comp).reshape(-1), jnp.full((256 - 3 * fibers,), -1, jnp.int32)]
    )
    meta = jnp.concatenate(
        [
            jnp.concatenate([attach_nucleus] * 4)[None, :256],
            target[None, :],
            jnp.zeros((6, 256), jnp.int32),
        ],
        axis=0,
    ).astype(F32)
    own = jnp.broadcast_to(
        jnp.stack([attach_nucleus, attach_node])[:, :, None], (2, fibers, 128)
    )
    vmem = pl.BlockSpec(memory_space=pltpu.VMEM)
    hbm = pl.BlockSpec(memory_space=pl.ANY)
    dma = pltpu.SemaphoreType.DMA
    pairs = tiles // 2
    scratch = [
        pltpu.VMEM(fiber_ops.shape, BF16),
        pltpu.VMEM(body_blocks.shape, BF16),
        pltpu.VMEM((tiles, 16, 256), F32),
        pltpu.VMEM((tiles, 16, 256), F32),
        pltpu.VMEM((tiles, 16, 256), F32),
        pltpu.VMEM((tiles, 8, 256), F32),
        pltpu.VMEM((tiles, 8, 256), F32),
        pltpu.VMEM((3, blocks, 128), F32),
        pltpu.VMEM((rows, 128), F32),
        pltpu.VMEM((rows, 128), F32),
        pltpu.VMEM((leaves + 2, 8, 128), F32),
        pltpu.VMEM((3, leaves + 4, 8, 128), F32),
        pltpu.VMEM((tiles, npad, cols), BF16),
        pltpu.VMEM((tiles, npad, 256), BF16),
        pltpu.VMEM((tiles, cols, 256), BF16),
        pltpu.VMEM((ITERS + 1, fibers, order), F32),
        pltpu.VMEM((ITERS + 1, npad, cols), F32),
        pltpu.VMEM((fibers, order), F32),
        pltpu.VMEM((npad, cols), F32),
        pltpu.VMEM((ITERS, 8, 128), F32),
        pltpu.VMEM((2, tiles, 8, 128), F32),
        pltpu.VMEM((2, grps, 8, 128), F32),
        dma((2,)),
        dma((tiles,)),
        dma((tiles,)),
        dma((tiles,)),
        dma((tiles,)),
        dma((tiles,)),
        dma((tiles,)),
        dma((tiles,)),
        dma((tiles,)),
        dma((pairs,)),
        dma((pairs,)),
        dma((2,)),
        dma((2,)),
        dma((2, tiles)),
        dma((2, tiles)),
        dma((2, grps)),
        dma((2, grps)),
    ]
    return pl.pallas_call(
        functools.partial(whole_kernel, tiles, grps),
        out_shape=(
            jax.ShapeDtypeStruct(rhs_fiber.shape, F32),
            jax.ShapeDtypeStruct(rhs_body.shape, F32),
        ),
        in_specs=[vmem, vmem, hbm, hbm] + [vmem] * 6,
        out_specs=(vmem, vmem),
        scratch_shapes=scratch,
        compiler_params=pltpu.CompilerParams(
            collective_id=0, has_side_effects=True, vmem_limit_bytes=VMEM_LIMIT
        ),
    )(
        rhs_fiber,
        rhs_body,
        fiber_ops,
        body_blocks,
        pos_nodes,
        send_index,
        leaf_index,
        near,
        meta,
        own,
    )


def solution(mesh):
    placed = (
        P(("grp", "tile"), None),
        P("grp", "tile"),
        P(("grp", "tile"), None, None),
        P("tile", None),
        P(None, ("grp", "tile")),
        P(("grp", "tile"), None),
        P(("grp", "tile"), None),
        P(("grp", "tile"), None),
        P(("grp", "tile")),
        P(("grp", "tile")),
    )
    return jax.shard_map(
        local,
        mesh=mesh,
        in_specs=placed,
        out_specs=(P(("grp", "tile"), None), P("grp", "tile")),
        check_vma=False,
    )
```

```python
import functools
import math

import jax
import jax.numpy as jnp
from jax import lax
from jax.experimental import pallas as pl
from jax.experimental.pallas import tpu as pltpu
from jax.sharding import PartitionSpec as P

FNODES = 64
BNODES = 1536
LEAF_PTS = 128
ITERS = 3

kappa_coef = 0.5
eps_square = 0.0025
stokes_coef = 1.0 / (16.0 * math.pi)

F32 = jnp.float32
BF16 = jnp.bfloat16
VMEM_LIMIT = 48 * 1024 * 1024


def iota(shape, dim):
    return lax.broadcasted_iota(jnp.int32, shape, dim)


def split2(x):
    hi = x.astype(BF16)
    return hi, (x - hi.astype(F32)).astype(BF16)


def gather_rows(halves, idx_ref, store):
    rows = halves[0].shape[0]
    lane = iota((rows, 128), 1)
    parts = []
    for c in range(3):
        keep = (lane < 64) if c % 2 == 0 else (lane >= 64)
        hi, low = split2(jnp.where(keep, halves[c // 2], 0.0))
        parts.append(jnp.concatenate([hi, low], axis=1))
    lhs = jnp.concatenate(parts, axis=0)
    blocks = idx_ref.shape[0]
    per = 4
    for b in range(0, blocks, per):
        idx = jnp.concatenate([idx_ref[b + k : b + k + 1, :] for k in range(per)], axis=1)
        hi_idx = idx >> 6
        lo_idx = idx & 63
        one = jnp.where(iota((64, per * 128), 0) == lo_idx, 1.0, 0.0).astype(BF16)
        table = jnp.concatenate([one] * 4, axis=0)
        picked = jnp.dot(lhs, table, preferred_element_type=F32)
        mask = iota((rows, per * 128), 0) == hi_idx
        for c in range(3):
            row = jnp.sum(
                jnp.where(mask, picked[c * rows : (c + 1) * rows], 0.0), axis=0, keepdims=True
            )
            for k in range(per):
                store(c, b + k, row[:, k * 128 : (k + 1) * 128])


def gather_exact(halves, idx_ref, store, add):
    gather_rows(halves, idx_ref, store)
    rest = []
    for x in halves:
        hi, low = split2(x)
        rest.append(x - hi.astype(F32) - low.astype(F32))
    gather_rows(rest, idx_ref, add)


def rows_to_halves(rows_ref, first_ref, second_ref):
    x0, x1, x2 = rows_ref[0], rows_ref[1], rows_ref[2]
    n = x0.shape[0]
    low = iota(x0.shape, 1) < 64
    first_ref[pl.ds(0, n, stride=2), :] = jnp.where(low, x0, pltpu.roll(x1, 64, 1))
    first_ref[pl.ds(1, n, stride=2), :] = jnp.where(low, pltpu.roll(x0, 64, 1), x1)
    second_ref[pl.ds(0, n, stride=2), :] = jnp.where(low, x2, 0.0)
    second_ref[pl.ds(1, n, stride=2), :] = jnp.where(low, pltpu.roll(x2, 64, 1), 0.0)


def halves_to_rows(first_ref, second_ref, rows_ref):
    n = rows_ref.shape[1]
    low = iota((n, 128), 1) < 64
    h0 = first_ref[pl.ds(0, n, stride=2), :]
    h1 = first_ref[pl.ds(1, n, stride=2), :]
    g0 = second_ref[pl.ds(0, n, stride=2), :]
    g1 = second_ref[pl.ds(1, n, stride=2), :]
    rows_ref[0] = jnp.where(low, h0, pltpu.roll(h1, 64, 1))
    rows_ref[1] = jnp.where(low, pltpu.roll(h0, 64, 1), h1)
    rows_ref[2] = jnp.where(low, g0, pltpu.roll(g1, 64, 1))


def scatter_halves(rows_ref, idx_ref, rows):
    blocks = idx_ref.shape[0]
    total = jnp.zeros((6 * rows, 128), F32)
    for b in range(0, blocks, 2):
        idx = jnp.concatenate([idx_ref[b : b + 1, :], idx_ref[b + 1 : b + 2, :]], axis=1)
        hi_idx = idx >> 6
        lo_idx = idx & 63
        one = jnp.where(iota((128, 256), 0) == lo_idx, 1.0, 0.0).astype(BF16)
        mask = jnp.where(iota((rows, 256), 0) == hi_idx, 1.0, 0.0)
        his, lows = [], []
        for c in range(3):
            x = jnp.concatenate(
                [rows_ref[c, b : b + 1, :], rows_ref[c, b + 1 : b + 2, :]], axis=1
            )
            hi, low = split2(x)
            his.append((mask * hi.astype(F32)).astype(BF16))
            lows.append((mask * low.astype(F32)).astype(BF16))
        lhs = jnp.concatenate(his + lows, axis=0)
        total += lax.dot_general(
            lhs, one, (((1,), (1,)), ((), ())), preferred_element_type=F32
        )
    parts = [
        total[c * rows : (c + 1) * rows] + total[(3 + c) * rows : (4 + c) * rows]
        for c in range(3)
    ]
    return parts[0] + pltpu.roll(parts[1], 64, 1), parts[2]


def total_of(x):
    return jnp.sum(jnp.sum(x, axis=0, keepdims=True), axis=1, keepdims=True)


def nt_dot(a, b):
    return lax.dot_general(a, b, (((1,), (1,)), ((), ())), preferred_element_type=F32)


def one_source(src_ref, near_ref, acc_ref, m):
    count = src_ref.shape[0]
    cols = jnp.transpose(src_ref[m])
    targets = []
    for d in range(3):
        t = (m + d - 1 + count) % count
        targets.append([src_ref[t, c : c + 1, :] for c in range(3)])
    sums = [[jnp.zeros((8, 128), F32) for _ in range(3)] for _ in range(3)]
    for s in range(LEAF_PTS // 8):
        col = [jnp.broadcast_to(cols[s * 8 : (s + 1) * 8, c : c + 1], (8, 128)) for c in range(6)]
        for d in range(3):
            dx = targets[d][0] - col[0]
            dy = targets[d][1] - col[1]
            dz = targets[d][2] - col[2]
            r2e = dx * dx + dy * dy + dz * dz + eps_square
            along = dx * col[3] + dy * col[4] + dz * col[5]
            inv = lax.rsqrt(r2e)
            cube = inv * inv * inv
            direct = (r2e + eps_square) * cube
            scaled = along * cube
            sums[d][0] += direct * col[3] + scaled * dx
            sums[d][1] += direct * col[4] + scaled * dy
            sums[d][2] += direct * col[5] + scaled * dz
    for d in range(3):
        for c in range(3):
            u = sums[d][c]
            if d != 1:
                u = u * near_ref[m, d // 2 : d // 2 + 1, :]
            acc_ref[c, m + d] += u


def whole_kernel(
    tiles,
    grps,
    rhs_f,
    rhs_b,
    ops_hbm,
    body_hbm,
    pos_ref,
    send_idx,
    leaf_idx,
    near_ref,
    meta_ref,
    own_ref,
    sol_f,
    sol_b,
    ops,
    raw,
    body,
    sbuf,
    rbuf,
    pbuf,
    bs,
    br,
    rows_ref,
    first_ref,
    second_ref,
    src_ref,
    acc_ref,
    full,
    pick,
    colpick,
    vf,
    vb,
    wf,
    wb,
    hs,
    ar1,
    ar2,
    local_sem,
    pos_s,
    pos_r,
    fwd_s,
    fwd_r,
    back_s,
    back_r,
    ag_s,
    ag_r,
    sib_s,
    sib_r,
    rim_s,
    rim_r,
    ar1_s,
    ar1_r,
    ar2_s,
    ar2_r,
):
    me = lax.axis_index("tile")
    grp = lax.axis_index("grp")
    rows = first_ref.shape[0]
    chunk = rows // tiles
    blocks = rows_ref.shape[1]
    leaves = blocks
    nuclei, cols = rhs_b.shape
    npad = full.shape[1]
    fibers, order = rhs_f.shape
    mesh_id = pl.DeviceIdType.MESH

    load_ops = pltpu.make_async_copy(ops_hbm, ops, local_sem.at[0])
    load_body = pltpu.make_async_copy(body_hbm, raw, local_sem.at[1])
    load_ops.start()
    load_body.start()

    barrier = pltpu.get_barrier_semaphore()
    for d in range(1, tiles):
        pl.semaphore_signal(
            barrier, inc=1, device_id=(grp, lax.rem(me + d, tiles)), device_id_type=mesh_id
        )
    for d in range(1, grps):
        pl.semaphore_signal(
            barrier, inc=1, device_id=(lax.rem(grp + d, grps), me), device_id_type=mesh_id
        )

    def to_tile(source, target, send_sem, recv_sem, peer):
        return pltpu.make_async_remote_copy(
            src_ref=source,
            dst_ref=target,
            send_sem=send_sem,
            recv_sem=recv_sem,
            device_id=(grp, peer),
            device_id_type=mesh_id,
        )

    def exchange(send, recv, send_sem, recv_sem):
        copies = []
        for d in range(1, tiles):
            peer = lax.rem(me + d, tiles)
            copies.append(
                to_tile(send.at[peer], recv.at[me], send_sem.at[d], recv_sem.at[d], peer)
            )
        return copies

    def reduce_start(p, value):
        ar1[p, me] = value
        copies = []
        for d in range(1, tiles):
            peer = lax.rem(me + d, tiles)
            copies.append(
                to_tile(ar1.at[p, me], ar1.at[p, me], ar1_s.at[p, d], ar1_r.at[p, d], peer)
            )
        for copy in copies:
            copy.start()
        return copies

    def reduce_end(p, copies):
        for copy in copies:
            copy.wait_recv()
        part = ar1[p, 0]
        for t in range(1, tiles):
            part = part + ar1[p, t]
        ar2[p, grp] = part
        second = []
        for d in range(1, grps):
            second.append(
                pltpu.make_async_remote_copy(
                    src_ref=ar2.at[p, grp],
                    dst_ref=ar2.at[p, grp],
                    send_sem=ar2_s.at[p, d],
                    recv_sem=ar2_r.at[p, d],
                    device_id=(lax.rem(grp + d, grps), me),
                    device_id_type=mesh_id,
                )
            )
        for copy in second:
            copy.start()
        for copy in second:
            copy.wait_recv()
        total = ar2[p, 0]
        for g in range(1, grps):
            total = total + ar2[p, g]
        for copy in copies + second:
            copy.wait_send()
        return total

    def keep_rows(c, b, piece):
        rows_ref[c, b : b + 1, :] = piece

    def add_rows(c, b, piece):
        rows_ref[c, b : b + 1, :] += piece

    def fill_send(extra, own_buf):
        rows_to_halves(rows_ref, first_ref, second_ref)
        for t in range(tiles):
            sbuf[t, 0:chunk, 0:128] = first_ref[t * chunk : (t + 1) * chunk, :]
            sbuf[t, 0:chunk, 128:256] = second_ref[t * chunk : (t + 1) * chunk, :]
            sbuf[t, 8:16, :] = extra
        own_buf[me] = sbuf[me]

    def received(buf):
        for t in range(tiles):
            first_ref[t * chunk : (t + 1) * chunk, :] = buf[t, 0:chunk, 0:128]
            second_ref[t * chunk : (t + 1) * chunk, :] = buf[t, 0:chunk, 128:256]

    gather_exact((pos_ref[:, :128], pos_ref[:, 128:]), send_idx, keep_rows, add_rows)
    fill_send(meta_ref[...], pbuf)
    pl.semaphore_wait(barrier, tiles + grps - 2)
    copies = exchange(sbuf, pbuf, pos_s, pos_r)
    for copy in copies:
        copy.start()
    norm = total_of(rhs_f[...] * rhs_f[...]) + total_of(rhs_b[...] * rhs_b[...])
    sums = reduce_start(0, jnp.broadcast_to(norm, (8, 128)))
    vf[...] = jnp.zeros_like(vf)
    vb[...] = jnp.zeros_like(vb)
    src_ref[...] = jnp.zeros_like(src_ref)
    for copy in copies:
        copy.wait_recv()
    received(pbuf)

    def keep_pos(c, b, piece):
        src_ref[1 + b, c : c + 1, :] = piece

    def add_pos(c, b, piece):
        src_ref[1 + b, c : c + 1, :] += piece

    gather_exact((first_ref[...], second_ref[...]), leaf_idx, keep_pos, add_pos)
    for t in range(tiles):
        nuc_row = pbuf[t, 8:9, :]
        col_row = pbuf[t, 9:10, :]
        pick[t] = jnp.where(iota((npad, 256), 0).astype(F32) == nuc_row, 1.0, 0.0).astype(BF16)
        my_col = (iota((cols, 256), 0) + me * cols).astype(F32)
        colpick[t] = jnp.where(my_col == col_row, 1.0, 0.0).astype(BF16)
    for copy in copies:
        copy.wait_send()
    load_body.wait()
    for t in range(tiles):
        body[t] = raw[:, t * cols : (t + 1) * cols]
    beta = jnp.sqrt(reduce_end(0, sums))[0:1]
    beta1 = beta[:, 0:1]
    vf[0] = rhs_f[...] / beta1
    vb[0, 0:nuclei, :] = rhs_b[...] / beta1
    load_ops.wait()

    def step(j, carry):
        p = (j + 1) % 2
        fiber = vf[j]
        full[me] = vb[j].astype(BF16)
        gather_rows((fiber[:, :128], fiber[:, 128:]), send_idx, keep_rows)
        end_pick = jnp.where(iota((8, order), 1) == iota((8, order), 0) * FNODES, 1.0, 0.0)
        end_pick = jnp.where(iota((8, order), 0) < 3, end_pick, 0.0).astype(BF16)
        hi, low = split2(fiber)
        ends = nt_dot(end_pick, hi) + nt_dot(end_pick, low)
        ends = jnp.concatenate([ends, jnp.zeros((8, 128 - fibers), F32)], axis=1)
        ends_row = jnp.concatenate(
            [ends[0:1] + pltpu.roll(ends, 64, 1)[1:2], ends[2:3]], axis=1
        )
        fill_send(jnp.broadcast_to(ends_row, (8, 256)), rbuf)
        forward = exchange(sbuf, rbuf, fwd_s, fwd_r)
        for copy in forward:
            copy.start()

        wide = jnp.concatenate([fiber, jnp.zeros((128 - fibers, order), F32)], axis=0)
        vec_t = jnp.transpose(wide).astype(BF16)

        def one_fiber(f, sofar):
            out = jnp.dot(ops[f], vec_t, preferred_element_type=F32)
            return jnp.where(iota((order, 128), 1) == f, out, sofar)

        prod = lax.fori_loop(0, fibers, one_fiber, jnp.zeros((order, 128), F32))
        wf[...] = fiber + jnp.transpose(prod)[:fibers]

        for copy in forward:
            copy.wait_recv()
        received(rbuf)

        def keep_force(c, b, piece):
            src_ref[1 + b, 3 + c : 4 + c, :] = piece

        gather_rows((first_ref[...], second_ref[...]), leaf_idx, keep_force)
        up = to_tile(
            src_ref.at[leaves], src_ref.at[0], rim_s.at[0], rim_r.at[0], lax.rem(me + 1, tiles)
        )
        down = to_tile(
            src_ref.at[1],
            src_ref.at[leaves + 1],
            rim_s.at[1],
            rim_r.at[1],
            lax.rem(me + tiles - 1, tiles),
        )
        up.start()
        down.start()
        sibling = me + 1 - 2 * (me % 2)
        spread = []
        for d in range(2, tiles, 2):
            peer = lax.rem(me + d, tiles)
            spread.append(to_tile(full.at[me], full.at[me], ag_s.at[d], ag_r.at[d], peer))
        paired = [to_tile(full.at[me], full.at[me], sib_s.at[0], sib_r.at[0], sibling)]
        for copy in spread + paired:
            copy.start()

        acc_ref[...] = jnp.zeros_like(acc_ref)

        def inside(m, c):
            one_source(src_ref, near_ref, acc_ref, m)
            return c

        lax.fori_loop(2, leaves, inside, 0)
        up.wait()
        down.wait()

        def edges(k, c):
            m = k % 2 + (k // 2) * leaves
            one_source(src_ref, near_ref, acc_ref, m)
            return c

        lax.fori_loop(0, 4, edges, 0)
        for c in range(3):
            rows_ref[c] = stokes_coef * jnp.sum(acc_ref[c, 2 : leaves + 2], axis=1)
        first, second = scatter_halves(rows_ref, leaf_idx, rows)
        for t in range(tiles):
            bs[t, 0:chunk, 0:128] = first[t * chunk : (t + 1) * chunk]
            bs[t, 0:chunk, 128:256] = second[t * chunk : (t + 1) * chunk]
        br[me] = bs[me]
        back = exchange(bs, br, back_s, back_r)
        for copy in back:
            copy.start()
        for i, copy in enumerate(spread):
            copy.wait_recv()
            got = lax.rem(me + tiles - 2 * (i + 1), tiles)
            paired.append(
                to_tile(full.at[got], full.at[got], sib_s.at[i + 1], sib_r.at[i + 1], sibling)
            )
            paired[-1].start()

        wb[...] = vb[j]
        for t in range(tiles):
            row = rbuf[t, 8:9, :]
            row_hi, row_low = split2(row)
            where = pick[t].astype(F32)
            lhs = jnp.concatenate(
                [(where * row_hi.astype(F32)).astype(BF16), (where * row_low.astype(F32)).astype(BF16)],
                axis=0,
            )
            pulled = nt_dot(lhs, colpick[t])
            wb[...] -= kappa_coef * (pulled[:npad] + pulled[npad:])
        for copy in paired:
            copy.wait_recv()

        def one_block(t, c):
            wb[...] += nt_dot(full[t], body[t])
            return c

        lax.fori_loop(0, tiles, one_block, 0)
        own_pick = jnp.where(iota((fibers, npad), 1) == own_ref[0, :, :npad], 1.0, 0.0).astype(BF16)
        node = own_ref[1, :, 0:1]
        felt = [jnp.zeros((fibers, 1), F32) for _ in range(3)]
        for t in range(tiles):
            picked = jnp.dot(own_pick, full[t], preferred_element_type=F32)
            at = iota((fibers, cols), 1) + t * cols
            for c in range(3):
                if t * cols < (c + 1) * BNODES and (t + 1) * cols > c * BNODES:
                    felt[c] += jnp.sum(
                        jnp.where(at == node + c * BNODES, picked, 0.0), axis=1, keepdims=True
                    )
        lane = iota((fibers, order), 1)
        for c in range(3):
            wf[...] -= kappa_coef * jnp.where(lane == c * FNODES, felt[c], 0.0)

        for copy in back:
            copy.wait_recv()
        received(br)
        halves_to_rows(first_ref, second_ref, rows_ref)
        first, second = scatter_halves(rows_ref, send_idx, rows)
        wf[:, 0:128] += first
        wf[:, 128:256] += second
        for copy in forward + back + spread + paired:
            copy.wait_send()

        fib, nuc = wf[...], wb[...]
        dots = [total_of(fib * vf[i]) + total_of(nuc * vb[i]) for i in range(3)]
        dots.append(total_of(fib * fib) + total_of(nuc * nuc))
        line = iota((8, 128), 0)
        value = jnp.zeros((8, 128), F32)
        for i in range(4):
            value = jnp.where(line == i, dots[i], value)
        total = reduce_end(p, reduce_start(p, value))
        length = jnp.sqrt(
            total[3:4]
            - (total[0:1] * total[0:1] + total[1:2] * total[1:2] + total[2:3] * total[2:3])
        )
        for i in range(3):
            h = total[i : i + 1, 0:1]
            fib = fib - h * vf[i]
            nuc = nuc - h * vb[i]
        vf[j + 1] = fib / length[:, 0:1]
        vb[j + 1] = nuc / length[:, 0:1]
        hs[j] = jnp.where(line == 3, length, total)
        return carry

    lax.fori_loop(0, ITERS, step, 0)

    h = [[None] * 3 for _ in range(4)]
    for j in range(3):
        for i in range(j + 1):
            h[i][j] = hs[j, i : i + 1, :]
        h[j + 1][j] = hs[j, 3:4, :]
    gram = [[None] * 3 for _ in range(3)]
    for i in range(3):
        for j in range(i + 1):
            value = jnp.zeros((1, 128), F32)
            for k in range(j + 2):
                value = value + h[k][i] * h[k][j]
            gram[i][j] = value
    l00 = jnp.sqrt(gram[0][0])
    l10 = gram[1][0] / l00
    l20 = gram[2][0] / l00
    l11 = jnp.sqrt(gram[1][1] - l10 * l10)
    l21 = (gram[2][1] - l20 * l10) / l11
    l22 = jnp.sqrt(gram[2][2] - l20 * l20 - l21 * l21)
    z0 = beta * h[0][0] / l00
    z1 = (beta * h[0][1] - l10 * z0) / l11
    z2 = (beta * h[0][2] - l20 * z0 - l21 * z1) / l22
    y2 = z2 / l22
    y1 = (z1 - l21 * y2) / l11
    y0 = (z0 - l10 * y1 - l20 * y2) / l00
    y0, y1, y2 = y0[:, 0:1], y1[:, 0:1], y2[:, 0:1]
    sol_f[...] = y0 * vf[0] + y1 * vf[1] + y2 * vf[2]
    body_out = y0 * vb[0] + y1 * vb[1] + y2 * vb[2]
    sol_b[...] = body_out[:nuclei]


def local(
    rhs_fiber,
    rhs_body,
    fiber_ops,
    body_op,
    positions,
    send_order,
    leaf_order,
    neighbours,
    attach_nucleus,
    attach_node,
):
    tiles = lax.axis_size("tile")
    grps = lax.axis_size("grp")
    me = lax.axis_index("tile")
    node_count = positions.shape[1]
    blocks = node_count // 128
    leaves = node_count // LEAF_PTS
    fibers, order = rhs_fiber.shape
    nuclei, cols = rhs_body.shape
    npad = -(-nuclei // 16) * 16
    rows = node_count // 64
    send_index = send_order.reshape(blocks, 128)
    leaf_index = leaf_order.reshape(blocks, 128)
    nb = neighbours.astype(F32)
    zero = jnp.zeros((1,), F32)
    leaf_id = jnp.arange(leaves)
    left = jnp.where((leaf_id == 0) & (me == 0), 0.0, nb[:, 0])
    right = jnp.where((leaf_id == leaves - 1) & (me == tiles - 1), 0.0, nb[:, 1])
    near = jnp.stack(
        [jnp.concatenate([zero, zero, right]), jnp.concatenate([left, zero, zero])]
        + [jnp.zeros((leaves + 2,), F32)] * 6,
        axis=1,
    )
    near = jnp.broadcast_to(near[:, :, None], (leaves + 2, 8, 128))
    pos_nodes = positions.reshape(3, rows, 64).transpose(1, 0, 2).reshape(rows, 192)
    pos_nodes = jnp.concatenate([pos_nodes, jnp.zeros((rows, 64), F32)], axis=1)
    comp = jnp.arange(3, dtype=jnp.int32)[:, None] * BNODES
    target = jnp.concatenate(
        [(attach_node[None, :] + comp).reshape(-1), jnp.full((256 - 3 * fibers,), -1, jnp.int32)]
    )
    meta = jnp.concatenate(
        [
            jnp.concatenate([attach_nucleus] * 4)[None, :256],
            target[None, :],
            jnp.zeros((6, 256), jnp.int32),
        ],
        axis=0,
    ).astype(F32)
    own = jnp.broadcast_to(
        jnp.stack([attach_nucleus, attach_node])[:, :, None], (2, fibers, 128)
    )
    vmem = pl.BlockSpec(memory_space=pltpu.VMEM)
    hbm = pl.BlockSpec(memory_space=pl.ANY)
    dma = pltpu.SemaphoreType.DMA
    pairs = tiles // 2
    scratch = [
        pltpu.VMEM(fiber_ops.shape, BF16),
        pltpu.VMEM(body_op.shape, BF16),
        pltpu.VMEM((tiles, cols, cols), BF16),
        pltpu.VMEM((tiles, 16, 256), F32),
        pltpu.VMEM((tiles, 16, 256), F32),
        pltpu.VMEM((tiles, 16, 256), F32),
        pltpu.VMEM((tiles, 8, 256), F32),
        pltpu.VMEM((tiles, 8, 256), F32),
        pltpu.VMEM((3, blocks, 128), F32),
        pltpu.VMEM((rows, 128), F32),
        pltpu.VMEM((rows, 128), F32),
        pltpu.VMEM((leaves + 2, 8, 128), F32),
        pltpu.VMEM((3, leaves + 4, 8, 128), F32),
        pltpu.VMEM((tiles, npad, cols), BF16),
        pltpu.VMEM((tiles, npad, 256), BF16),
        pltpu.VMEM((tiles, cols, 256), BF16),
        pltpu.VMEM((ITERS + 1, fibers, order), F32),
        pltpu.VMEM((ITERS + 1, npad, cols), F32),
        pltpu.VMEM((fibers, order), F32),
        pltpu.VMEM((npad, cols), F32),
        pltpu.VMEM((ITERS, 8, 128), F32),
        pltpu.VMEM((2, tiles, 8, 128), F32),
        pltpu.VMEM((2, grps, 8, 128), F32),
        dma((2,)),
        dma((tiles,)),
        dma((tiles,)),
        dma((tiles,)),
        dma((tiles,)),
        dma((tiles,)),
        dma((tiles,)),
        dma((tiles,)),
        dma((tiles,)),
        dma((pairs,)),
        dma((pairs,)),
        dma((2,)),
        dma((2,)),
        dma((2, tiles)),
        dma((2, tiles)),
        dma((2, grps)),
        dma((2, grps)),
    ]
    return pl.pallas_call(
        functools.partial(whole_kernel, tiles, grps),
        out_shape=(
            jax.ShapeDtypeStruct(rhs_fiber.shape, F32),
            jax.ShapeDtypeStruct(rhs_body.shape, F32),
        ),
        in_specs=[vmem, vmem, hbm, hbm] + [vmem] * 6,
        out_specs=(vmem, vmem),
        scratch_shapes=scratch,
        compiler_params=pltpu.CompilerParams(
            collective_id=0, has_side_effects=True, vmem_limit_bytes=VMEM_LIMIT
        ),
    )(
        rhs_fiber,
        rhs_body,
        fiber_ops,
        body_op,
        pos_nodes,
        send_index,
        leaf_index,
        near,
        meta,
        own,
    )


def solution(mesh):
    placed = (
        P(("grp", "tile"), None),
        P("grp", "tile"),
        P(("grp", "tile"), None, None),
        P("tile", None),
        P(None, ("grp", "tile")),
        P(("grp", "tile"), None),
        P(("grp", "tile"), None),
        P(("grp", "tile"), None),
        P(("grp", "tile")),
        P(("grp", "tile")),
    )
    return jax.shard_map(
        local,
        mesh=mesh,
        in_specs=placed,
        out_specs=(P(("grp", "tile"), None), P("grp", "tile")),
        check_vma=False,
    )
```
